32 devices in a mesh: leaf: 4 (over z), panel: 8 (over y, x, core).
Axes of the slice: x: 2, y: 2, z: 4, core: 2. Of those that a mesh axis runs over, the one named last changes fastest.
Arguments:
- right_sides: float32 [4, 256, 32, 256], P('leaf', 'panel'), may hold values from -6 to 6
- inverse: float32 [4, 256, 256, 256], P('leaf', 'panel'), as said below
- coupling: float32 [4, 256, 256, 256], P('leaf', 'panel'), may hold values from -0.25 to 0.25
- owner_map: int32 [4, 256, 1], P('leaf', 'panel'), may hold values from 0 to 7; in each aligned block of 32 rows (0 to 31, 32 to 63, ..., all dimensions but the last counted through in order) at most 8 rows name the same one
- parent_slot: int32 [4, 256], P('leaf', 'panel'), may hold values from 0 to 31
Outputs:
- forward_solution: float32 [4, 256, 32, 256], P('leaf', 'panel')
- backward_solution: float32 [4, 256, 32, 256], P('leaf', 'panel')
The draws below stay inside these ranges and needn't reach their ends.
Inputs may be any that keep to these rules, and one draw needn't show every extreme that they name: `owner_map`: within the 32 supernodes of one device no owner is named more than 8 times, and some owner is named exactly that often; entries of the top level are not read. `inverse`: each block is upper triangular with a positive diagonal.
All inputs are finite; a program needn't handle non-finite values.
Results may differ from the reference program's by a relative error of at most 0.0001.
Values sent between devices are 32-bit elements; how exact they have to be, the bound alone decides.
A program may use at most 128 MiB of HBM per device.

```python
import math
import jax
import jax.numpy as jnp
import numpy as np
from jax import lax

BLOCK = 256
RHS_COLS = 32
NODE_DEV = 32
LEVELS = 4
NODES = 256
CAPACITY = 8
N_PANEL = 8


def draw_inverse(key, part):
    first_key, second_key = jax.random.split(jax.random.fold_in(key, 17))
    shape = (LEVELS, NODES, BLOCK, BLOCK)
    row_index = lax.broadcasted_iota(jnp.int32, (BLOCK, BLOCK), 0)
    col_index = lax.broadcasted_iota(jnp.int32, (BLOCK, BLOCK), 1)
    diagonal = jax.random.uniform(first_key, shape, jnp.float32, 0.6, 1.6)
    above = jax.random.normal(second_key, shape, jnp.float32) * (0.5 / math.sqrt(BLOCK))
    return jnp.where(row_index == col_index, diagonal, jnp.where(col_index > row_index, above, 0.0)).astype(jnp.float32)


def plant(entries, key, low, top_value):
    longest = entries.shape.index(max(entries.shape))
    spots = []
    for shift in (0, 1):
        where = [jax.random.randint(jax.random.fold_in(key, axis), (), 0, length) for axis, length in enumerate(entries.shape)]
        where[longest] = (where[longest] + shift) % entries.shape[longest]
        spots.append(tuple(where))
    return entries.at[spots[0]].set(low).at[spots[1]].set(top_value)


def block_levels(key, extent, pieces, smallest, top_value):
    loudness = 1.0
    for axis_at, parts in pieces:
        heights = jax.random.uniform(jax.random.fold_in(jax.random.fold_in(key, 6), axis_at), (parts,), jnp.float32, smallest / len(pieces), top_value / len(pieces))
        loudness = loudness * jnp.repeat(jnp.exp(heights), extent[axis_at] // parts).reshape((-1,) + (1,) * (len(extent) - 1 - axis_at))
    return loudness


def shared_out(own_key, own, number, rows, number_of, top, limit, skew):
    order = jax.random.permutation(own_key, number_of)
    packed, ordinary = load_shares(number_of, rows * top, limit, skew, True), load_shares(number_of, rows * top, limit, skew, False)
    places = jnp.arange(number_of)

    def named(lengths, rotation):
        used = int((lengths > 0).sum())
        fixed = max(1, used // 4)
        passed = fixed + (places - fixed + rotation * (used - fixed)) % max(1, number_of - fixed)
        return jnp.zeros((number_of,), jnp.int32).at[order[jnp.where(places < fixed, places, passed)]].set(jnp.asarray(lengths, jnp.int32))

    lengths = jnp.where(number % 4 == 0, named(packed, number // 4), named(ordinary, number - number // 4 - 1))
    mixed = jax.random.permutation(jax.random.fold_in(own, 3), number_of)
    giver, sink = mixed[0:number_of // 2 * 2:2], mixed[1:number_of // 2 * 2:2]
    room = jnp.minimum(lengths[giver] - 1, limit - lengths[sink]) // 2
    room = jnp.where((giver == order[0]) | (sink == order[0]) | (lengths[sink] == 0), 0, jnp.maximum(room, 0))
    passed = jax.random.randint(jax.random.fold_in(own, 4), (number_of // 2,), 0, 1 << 20) % (room + 1)
    lengths = lengths.at[giver].add(-passed).at[sink].add(passed)
    labels = jnp.searchsorted(jnp.cumsum(lengths), jnp.arange(rows * top), side="right").astype(jnp.int32)
    grid = labels.reshape(top, rows).T
    grid = grid[jax.random.permutation(jax.random.fold_in(own, 1), rows)]
    rotation = jax.random.randint(jax.random.fold_in(own, 2), (rows, 1), 0, top)
    return jnp.take_along_axis(grid, (jnp.arange(top)[None, :] + rotation) % top, axis=1)


def load_shares(amount, total, reach, slope, full):
    portions = [(1 << 20) // math.isqrt(grade ** slope) + 1 for grade in range(1, amount + 1)]
    largest = reach if full else min(reach, max(-(-total // amount), total * portions[0] // sum(portions)))
    least = 1 if total - largest >= amount - 1 else 0
    holding, surplus = [largest] + [least] * (amount - 1), total - largest - least * (amount - 1)
    while surplus > 0:
        free = [i for i in range(1, amount) if holding[i] < largest] or [i for i in range(1, amount) if holding[i] < reach]
        whole, left = sum([portions[i] for i in free]), surplus
        for i in free:
            addition = min(reach - holding[i], max(1, left * portions[i] // whole), surplus)
            holding[i] = holding[i] + addition
            surplus = surplus - addition
    return np.array(holding)


def centred(own_key, shape, spread, most, cuts=(), dtype=jnp.bfloat16):
    level = block_levels(own_key, shape, cuts, -0.22, 0.18) if cuts else 1.0
    drawn = jax.random.normal(own_key, shape, jnp.float32) * spread * level
    return jnp.minimum(jnp.maximum(drawn, -most), most).astype(dtype)


def setup_inputs(seed: int = 0) -> dict:
    seeds = jax.random.split(jax.random.key(seed), 6)
    right_sides = centred(seeds[0], (LEVELS, NODES, RHS_COLS, BLOCK), 1.0, 6.0, ((0, 4), (1, 8)), jnp.float32)
    inverse = draw_inverse(jax.random.fold_in(seeds[5], 71), 0)
    coupling = centred(seeds[2], (LEVELS, NODES, BLOCK, BLOCK), (2 * BLOCK) ** -0.5, 0.25, ((0, 4), (1, 8)), jnp.float32)
    owner_map_keys = jax.random.split(jax.random.fold_in(seeds[3], 1), LEVELS * NODES // NODE_DEV)
    owner_map_turns = jax.random.permutation(jax.random.fold_in(seeds[3], 3), LEVELS * NODES // NODE_DEV)
    owner_map = jax.vmap(lambda own, number: shared_out(jax.random.fold_in(seeds[3], 2), own, number, NODE_DEV, N_PANEL, 1, CAPACITY, 2))(owner_map_keys, owner_map_turns).reshape((LEVELS, NODES, 1))
    parent_slot = plant(jax.random.randint(seeds[4], (LEVELS, NODES), 0, NODE_DEV), jax.random.fold_in(seeds[4], 1), 0, NODE_DEV - 1).astype(jnp.int32)
    return dict(right_sides=right_sides, inverse=inverse, coupling=coupling, owner_map=owner_map, parent_slot=parent_slot)


def reference(right_sides, inverse, coupling, owner_map, parent_slot):
    highest = lax.Precision.HIGHEST
    parent = (owner_map[:, :, 0] * NODE_DEV + parent_slot).astype(jnp.int32)
    incoming = jnp.zeros(right_sides.shape[1:], jnp.float32)
    forward_list = []
    for level in range(LEVELS):
        solved = jnp.einsum('nrw,nwv->nrv', right_sides[level] - incoming, inverse[level], precision=highest)
        forward_list.append(solved)
        if level < LEVELS - 1:
            updates = jnp.einsum('nrw,nwv->nrv', solved, coupling[level], precision=highest)
            incoming = jax.ops.segment_sum(updates, parent[level], num_segments=NODES)
    backward_list = [None] * LEVELS
    above = jnp.einsum('nrw,nvw->nrv', forward_list[LEVELS - 1], inverse[LEVELS - 1], precision=highest)
    backward_list[LEVELS - 1] = above
    for level in range(LEVELS - 2, -1, -1):
        from_parent = above[parent[level]]
        lowered = jnp.einsum('nrv,nwv->nrw', from_parent, coupling[level], precision=highest)
        above = jnp.einsum('nrw,nvw->nrv', forward_list[level] - lowered, inverse[level], precision=highest)
        backward_list[level] = above
    return jnp.stack(forward_list), jnp.stack(backward_list)
```

```python
import functools

import jax
import jax.numpy as jnp
from jax import lax
from jax.experimental import pallas as pl
from jax.experimental.pallas import tpu as pltpu
from jax.sharding import PartitionSpec as P

MESH = pl.DeviceIdType.MESH
ROWS = 8
WCHUNK = 4


def split_rows(x):
    high = x.astype(jnp.bfloat16).astype(jnp.float32)
    return jnp.concatenate([high, x - high], axis=0).astype(jnp.bfloat16)


def times(x, weights):
    parts = split_rows(x)
    parts = jnp.concatenate([parts, parts], axis=1)
    out = jnp.dot(parts, weights, preferred_element_type=jnp.float32)
    return out[:ROWS] + out[ROWS:]


def times_transposed(x, weights):
    parts = split_rows(x)
    out = lax.dot_general(parts, weights, (((1,), (1,)), ((), ())), preferred_element_type=jnp.float32)
    half = out.shape[1] // 2
    return (out[:ROWS, :half] + out[ROWS:, :half]) + (out[:ROWS, half:] + out[ROWS:, half:])


def kernel(levels, panels, nodes, blocks, width, cap, *refs):
    meta, given, inverse, coupling, fwd_out, bwd_out = refs[:6]
    refs = list(refs[6:])
    take = lambda count: [refs.pop(0) for _ in range(count)]
    inv32, cpl32, inv, cpl, gbuf, fsol, bsol, upd, prefix, send_up, sums, got_sums, send_down = take(13)
    got_up, got_down, got_above = take(blocks), take(blocks), take(blocks)
    w_sem, g_sem, o_sem, up_s, up_r, z_s, z_r, dn_s, dn_r, b_s, b_r = take(11)

    slots = panels * cap
    m_send, m_order, m_cont, m_pos, m_last, m_slot = 0, slots, 2 * slots, 3 * slots, 4 * slots, 4 * slots + nodes
    level = lax.axis_index("leaf")
    me = lax.axis_index("panel")
    chunk = ROWS
    chunks = nodes // chunk
    wchunks = nodes // WCHUNK
    below_top = level < levels - 1
    above_bottom = level > 0

    def given_copy(b):
        return pltpu.make_async_copy(given.at[0, :, pl.ds(b * ROWS, ROWS), :], gbuf.at[b], g_sem.at[b])

    def weight_copy(which, c):
        source, target = ((inverse, inv32), (coupling, cpl32))[which]
        span = pl.ds(c * WCHUNK, WCHUNK)
        return pltpu.make_async_copy(source.at[0, span], target.at[span], w_sem.at[which, c])

    def out_copy(which, b):
        source, target = ((fsol, fwd_out), (bsol, bwd_out))[which]
        return pltpu.make_async_copy(source.at[b], target.at[0, :, pl.ds(b * ROWS, ROWS), :], o_sem.at[which, b])

    def spread_copy(b, buffer, target, send, recv, owner):
        return pltpu.make_async_remote_copy(
            src_ref=buffer.at[b, pl.ds(owner * cap, cap)], dst_ref=target.at[pl.ds(me * cap, cap)],
            send_sem=send.at[b], recv_sem=recv.at[b], device_id=(level, owner), device_id_type=MESH)

    def up_copy(b, c):
        span = pl.ds(c * chunk, chunk)
        return pltpu.make_async_remote_copy(
            src_ref=sums.at[b, span], dst_ref=got_sums.at[b, span],
            send_sem=z_s.at[b], recv_sem=z_r.at[b, c], device_id=(level + 1, me), device_id_type=MESH)

    def down_copy(b, c):
        span = pl.ds(c * chunk, chunk)
        return pltpu.make_async_remote_copy(
            src_ref=bsol.at[b, span], dst_ref=got_above[b].at[span],
            send_sem=b_s.at[b], recv_sem=b_r.at[b], device_id=(level - 1, me), device_id_type=MESH)

    def wait_bytes(ref, sem):
        pltpu.make_async_copy(ref, ref, sem).wait()

    given_copy(0).start()
    for c in range(wchunks):
        weight_copy(0, c).start()
        weight_copy(1, c).start()
    for b in range(1, blocks):
        given_copy(b).start()

    barrier = pltpu.get_barrier_semaphore()

    def greet(d, carry):
        pl.semaphore_signal(barrier, inc=1, device_id=(level, lax.rem(me + d, panels)), device_id_type=MESH)
        return carry

    lax.fori_loop(1, panels, greet, 0)

    @pl.when(below_top)
    def _():
        pl.semaphore_signal(barrier, inc=1, device_id=(level + 1, me), device_id_type=MESH)

    @pl.when(above_bottom)
    def _():
        pl.semaphore_signal(barrier, inc=1, device_id=(level - 1, me), device_id_type=MESH)

    vertical = jnp.where(below_top, 1, 0) + jnp.where(above_bottom, 1, 0)
    pl.semaphore_wait(barrier, panels - 1 + vertical)

    @pl.when(level == 0)
    def _():
        got_sums[...] = jnp.zeros_like(got_sums)

    prefix[slots] = jnp.zeros((ROWS, width), jnp.float32)

    def forward_nodes(b, first, count):
        for i in range(count):
            n = first + i
            x = times(gbuf[b, n] - got_sums[b, n], inv[n])
            fsol[b, n] = x
            upd[n] = times(x, cpl[n])

    given_copy(0).wait()

    def prepare(c, carry):
        for which, (source, target) in enumerate(((inv32, inv), (cpl32, cpl))):
            weight_copy(which, c).wait()
            for i in range(WCHUNK):
                n = c * WCHUNK + i
                for r in range(0, width, 64):
                    w = source[n, r:r + 64, :]
                    high = w.astype(jnp.bfloat16)
                    target[n, r:r + 64, :] = high
                    target[n, width + r:width + r + 64, :] = (w - high.astype(jnp.float32)).astype(jnp.bfloat16)

        @pl.when(level == 0)
        def _():
            forward_nodes(0, c * WCHUNK, WCHUNK)

        return carry

    lax.fori_loop(0, wchunks, prepare, 0)

    def forward(b):
        if b > 0:
            given_copy(b).wait()

        def one(c, carry):
            @pl.when(above_bottom)
            def _():
                wait_bytes(got_sums.at[b, pl.ds(c * chunk, chunk)], z_r.at[b, c])

            forward_nodes(b, c * chunk, chunk)
            return carry

        lax.fori_loop(0, chunks, one, 0)

    def spread(b, source, base, buffer, target, send, recv):
        for k in range(cap):
            target[me * cap + k] = source[meta[base + me * cap + k]]

        def one(d, carry):
            owner = lax.rem(me + d, panels)
            for k in range(cap):
                buffer[b, owner * cap + k] = source[meta[base + owner * cap + k]]
            spread_copy(b, buffer, target, send, recv, owner).start()
            return carry

        lax.fori_loop(1, panels, one, 0)

    def add_up(b):
        wait_bytes(got_up[b].at[pl.ds(0, slots - cap)], up_r.at[b])

        def run(j8, acc):
            for i in range(8):
                j = j8 * 8 + i
                acc = jnp.where(meta[m_cont + j] > 0, acc, 0.0) + got_up[b][meta[m_order + j]]
                prefix[j] = acc
            return acc

        lax.fori_loop(0, slots // 8, run, jnp.zeros((ROWS, width), jnp.float32))

        def one(c, carry):
            for i in range(chunk):
                m = c * chunk + i
                sums[b, m] = prefix[meta[m_last + m]]
            up_copy(b, c).start()
            return carry

        lax.fori_loop(0, chunks, one, 0)

    def top(b):
        def one(c, carry):
            wait_bytes(got_sums.at[b, pl.ds(c * chunk, chunk)], z_r.at[b, c])
            for i in range(chunk):
                n = c * chunk + i
                x = times(gbuf[b, n] - got_sums[b, n], inv[n])
                fsol[b, n] = x
                bsol[b, n] = times_transposed(x, inv[n])
            down_copy(b, c).start()
            return carry

        lax.fori_loop(0, chunks, one, 0)

    def hand_down(b):
        wait_bytes(got_above[b], b_r.at[b])
        spread(b, got_above[b], m_pos, send_down, got_down[b], dn_s, dn_r)

    def backward(b):
        wait_bytes(got_down[b].at[pl.ds(0, slots - cap)], dn_r.at[b])

        def one(c, carry):
            for i in range(chunk):
                n = c * chunk + i
                low = times_transposed(got_down[b][meta[m_slot + n]], cpl[n])
                bsol[b, n] = times_transposed(fsol[b, n] - low, inv[n])

            @pl.when(above_bottom)
            def _():
                down_copy(b, c).start()

            return carry

        lax.fori_loop(0, chunks, one, 0)
        out_copy(1, b).start()

    @pl.when(below_top)
    def _():
        for b in range(blocks + 1):
            if b < blocks:
                if b == 0:
                    @pl.when(above_bottom)
                    def _():
                        forward(0)
                else:
                    forward(b)
                spread(b, upd, m_send, send_up, got_up[b], up_s, up_r)
                out_copy(0, b).start()
            if b > 0:
                add_up(b - 1)
        for b in range(blocks + 1):
            if b < blocks:
                hand_down(b)
            if b > 0:
                backward(b - 1)
        for b in range(blocks):
            wait_bytes(send_up.at[b, pl.ds(0, slots - cap)], up_s.at[b])
            wait_bytes(send_down.at[b, pl.ds(0, slots - cap)], dn_s.at[b])
            wait_bytes(sums.at[b], z_s.at[b])

    @pl.when(level == levels - 1)
    def _():
        for b in range(blocks):
            if b > 0:
                given_copy(b).wait()
            top(b)
            out_copy(0, b).start()
            out_copy(1, b).start()

    @pl.when(above_bottom)
    def _():
        for b in range(blocks):
            wait_bytes(bsol.at[b], b_s.at[b])

    for b in range(blocks):
        out_copy(0, b).wait()
        out_copy(1, b).wait()


def places(owners, positions, panels, cap):
    nodes = owners.shape[0]
    slots = panels * cap
    i32 = jnp.int32
    node = jnp.arange(nodes, dtype=i32)
    slot = jnp.arange(slots, dtype=i32)
    same = (owners[:, None] == owners[None, :]) & (node[None, :] < node[:, None])
    dest = owners * cap + jnp.sum(same.astype(i32), axis=1)
    hit = slot[:, None] == dest[None, :]
    send = jnp.sum(jnp.where(hit, node[None, :], 0), axis=1)
    ids = nodes - jnp.sum(jnp.where(hit, nodes - positions[None, :], 0), axis=1)
    key = lax.all_to_all(ids, "panel", split_axis=0, concat_axis=0, tiled=True)
    ahead = (key[None, :] < key[:, None]) | ((key[None, :] == key[:, None]) & (slot[None, :] < slot[:, None]))
    rank = jnp.sum(ahead.astype(i32), axis=1)
    placed = rank[None, :] == slot[:, None]
    order = jnp.sum(jnp.where(placed, slot[None, :], 0), axis=1)
    cont = jnp.max(jnp.where(ahead & (key[None, :] == key[:, None]), 1, 0), axis=1)
    cont = jnp.sum(jnp.where(placed, cont[None, :], 0), axis=1)
    mine = key[None, :] == node[:, None]
    last = jnp.max(jnp.where(mine, rank[None, :], -1), axis=1)
    last = jnp.where(last < 0, slots, last)
    return jnp.concatenate([send, order, cont, jnp.minimum(key, nodes - 1), last, dest]).astype(i32)


def body(right_sides, inverse, coupling, owner_map, parent_slot):
    levels = lax.axis_size("leaf")
    panels = lax.axis_size("panel")
    nodes, total_cols, width = right_sides.shape[1:]
    cap = max(2, 2 * nodes // panels)
    slots = panels * cap
    blocks = total_cols // ROWS
    meta = places(owner_map[0, :, 0], parent_slot[0], panels, cap)
    tile = (ROWS, width)
    f32, bf16 = jnp.float32, jnp.bfloat16
    vmem = pltpu.VMEM
    dma = pltpu.SemaphoreType.DMA
    chunks = nodes // ROWS
    scratch = [
        vmem((nodes, width, width), f32), vmem((nodes, width, width), f32),
        vmem((nodes, 2 * width, width), bf16), vmem((nodes, 2 * width, width), bf16),
        vmem((blocks, nodes) + tile, f32), vmem((blocks, nodes) + tile, f32), vmem((blocks, nodes) + tile, f32),
        vmem((nodes,) + tile, f32), vmem((slots + 1,) + tile, f32),
        vmem((blocks, slots) + tile, f32), vmem((blocks, nodes) + tile, f32), vmem((blocks, nodes) + tile, f32),
        vmem((blocks, slots) + tile, f32),
    ]
    scratch += [vmem((slots,) + tile, f32) for _ in range(2 * blocks)]
    scratch += [vmem((nodes,) + tile, f32) for _ in range(blocks)]
    scratch += [
        dma((2, nodes // WCHUNK)), dma((blocks,)), dma((2, blocks)),
        dma((blocks,)), dma((blocks,)), dma((blocks,)), dma((blocks, chunks)),
        dma((blocks,)), dma((blocks,)), dma((blocks,)), dma((blocks,)),
    ]
    out = jax.ShapeDtypeStruct(right_sides.shape, f32)
    anywhere = pl.BlockSpec(memory_space=pl.ANY)
    return pl.pallas_call(
        functools.partial(kernel, levels, panels, nodes, blocks, width, cap),
        out_shape=(out, out),
        in_specs=[pl.BlockSpec(memory_space=pltpu.SMEM), anywhere, anywhere, anywhere],
        out_specs=(anywhere, anywhere),
        scratch_shapes=scratch,
        compiler_params=pltpu.CompilerParams(
            collective_id=0, has_side_effects=True, vmem_limit_bytes=60 * 1024 * 1024
        ),
    )(meta, right_sides, inverse, coupling)


def solution(mesh):
    in_specs = (
        P("leaf", "panel", None, None),
        P("leaf", "panel", None, None),
        P("leaf", "panel", None, None),
        P("leaf", "panel", None),
        P("leaf", "panel"),
    )
    out_specs = (P("leaf", "panel", None, None), P("leaf", "panel", None, None))
    return jax.shard_map(body, mesh=mesh, in_specs=in_specs, out_specs=out_specs, check_vma=False)
```

```python
import functools

import jax
import jax.numpy as jnp
from jax import lax
from jax.experimental import pallas as pl
from jax.experimental.pallas import tpu as pltpu
from jax.sharding import PartitionSpec as P

MESH = pl.DeviceIdType.MESH
ROWS = 8
WCHUNK = 4
STAGED = 4


def split_rows(x):
    high = x.astype(jnp.bfloat16).astype(jnp.float32)
    return jnp.concatenate([high, x - high], axis=0).astype(jnp.bfloat16)


def times(x, weights):
    parts = split_rows(x)
    parts = jnp.concatenate([parts, parts], axis=1)
    out = jnp.dot(parts, weights, preferred_element_type=jnp.float32)
    return out[:ROWS] + out[ROWS:]


def kernel(levels, panels, nodes, blocks, width, cap, *refs):
    meta, given, inverse, coupling, fwd_out, bwd_out = refs[:6]
    refs = list(refs[6:])
    take = lambda count: [refs.pop(0) for _ in range(count)]
    inv32, cpl32, inv, cpl, inv_t, cpl_t, gbuf, fsol, bsol, upd, prefix, send_up, sums, got_sums, send_down = take(15)
    got_up, got_down, got_above = take(blocks), take(blocks), take(blocks)
    w_sem, g_sem, o_sem, up_s, up_r, z_s, z_r, dn_s, dn_r, b_s, b_r = take(11)

    slots = panels * cap
    m_send, m_order, m_cont, m_pos, m_last, m_slot = 0, slots, 2 * slots, 3 * slots, 4 * slots, 4 * slots + nodes
    level = lax.axis_index("leaf")
    me = lax.axis_index("panel")
    chunk = ROWS
    chunks = nodes // chunk
    wchunks = nodes // WCHUNK
    below_top = level < levels - 1
    above_bottom = level > 0

    def given_copy(b):
        return pltpu.make_async_copy(given.at[0, :, pl.ds(b * ROWS, ROWS), :], gbuf.at[b], g_sem.at[b])

    def weight_copy(which, c):
        source, target = ((inverse, inv32), (coupling, cpl32))[which]
        place = lax.rem(c, STAGED) * WCHUNK
        return pltpu.make_async_copy(
            source.at[0, pl.ds(c * WCHUNK, WCHUNK)], target.at[pl.ds(place, WCHUNK)], w_sem.at[which, c])

    def out_copy(which, b):
        source, target = ((fsol, fwd_out), (bsol, bwd_out))[which]
        return pltpu.make_async_copy(source.at[b], target.at[0, :, pl.ds(b * ROWS, ROWS), :], o_sem.at[which, b])

    def spread_copy(b, buffer, target, send, recv, owner):
        return pltpu.make_async_remote_copy(
            src_ref=buffer.at[b, pl.ds(owner * cap, cap)], dst_ref=target.at[pl.ds(me * cap, cap)],
            send_sem=send.at[b], recv_sem=recv.at[b], device_id=(level, owner), device_id_type=MESH)

    def up_copy(b, c):
        span = pl.ds(c * chunk, chunk)
        return pltpu.make_async_remote_copy(
            src_ref=sums.at[b, span], dst_ref=got_sums.at[b, span],
            send_sem=z_s.at[b], recv_sem=z_r.at[b, c], device_id=(level + 1, me), device_id_type=MESH)

    def down_copy(b, c):
        span = pl.ds(c * chunk, chunk)
        return pltpu.make_async_remote_copy(
            src_ref=bsol.at[b, span], dst_ref=got_above[b].at[span],
            send_sem=b_s.at[b], recv_sem=b_r.at[b], device_id=(level - 1, me), device_id_type=MESH)

    def wait_bytes(ref, sem):
        pltpu.make_async_copy(ref, ref, sem).wait()

    given_copy(0).start()
    for c in range(min(STAGED, wchunks)):
        weight_copy(0, c).start()
        weight_copy(1, c).start()
    for b in range(1, blocks):
        given_copy(b).start()

    barrier = pltpu.get_barrier_semaphore()

    def greet(d, carry):
        pl.semaphore_signal(barrier, inc=1, device_id=(level, lax.rem(me + d, panels)), device_id_type=MESH)
        return carry

    lax.fori_loop(1, panels, greet, 0)

    @pl.when(below_top)
    def _():
        pl.semaphore_signal(barrier, inc=1, device_id=(level + 1, me), device_id_type=MESH)

    @pl.when(above_bottom)
    def _():
        pl.semaphore_signal(barrier, inc=1, device_id=(level - 1, me), device_id_type=MESH)

    vertical = jnp.where(below_top, 1, 0) + jnp.where(above_bottom, 1, 0)
    pl.semaphore_wait(barrier, panels - 1 + vertical)

    @pl.when(level == 0)
    def _():
        got_sums[...] = jnp.zeros_like(got_sums)

    prefix[slots] = jnp.zeros((ROWS, width), jnp.float32)

    def forward_nodes(b, first, count):
        for i in range(count):
            n = first + i
            x = times(gbuf[b, n] - got_sums[b, n], inv[n])
            fsol[b, n] = x
            upd[n] = times(x, cpl[n])

    given_copy(0).wait()

    def prepare(c, carry):
        for which, (source, target) in enumerate(((inv32, inv), (cpl32, cpl))):
            weight_copy(which, c).wait()
            for i in range(WCHUNK):
                n = c * WCHUNK + i
                for r in range(0, width, 64):
                    w = source[lax.rem(c, STAGED) * WCHUNK + i, r:r + 64, :]
                    high = w.astype(jnp.bfloat16)
                    target[n, r:r + 64, :] = high
                    target[n, width + r:width + r + 64, :] = (w - high.astype(jnp.float32)).astype(jnp.bfloat16)

        @pl.when(c + STAGED < wchunks)
        def _():
            weight_copy(0, c + STAGED).start()
            weight_copy(1, c + STAGED).start()

        @pl.when(level == 0)
        def _():
            forward_nodes(0, c * WCHUNK, WCHUNK)

        return carry

    lax.fori_loop(0, wchunks, prepare, 0)

    def turn(n, carry):
        for source, target in ((inv, inv_t), (cpl, cpl_t)):
            for r in (0, width):
                target[n, r:r + width, :] = source[n, r:r + width, :].T
        return carry

    @pl.when(above_bottom)
    def _():
        lax.fori_loop(0, nodes, turn, 0)

    def forward(b):
        if b > 0:
            given_copy(b).wait()

        def one(c, carry):
            @pl.when(above_bottom)
            def _():
                wait_bytes(got_sums.at[b, pl.ds(c * chunk, chunk)], z_r.at[b, c])

            forward_nodes(b, c * chunk, chunk)
            return carry

        lax.fori_loop(0, chunks, one, 0)

    def spread(b, source, base, buffer, target, send, recv):
        for k in range(cap):
            target[me * cap + k] = source[meta[base + me * cap + k]]

        def one(d, carry):
            owner = lax.rem(me + d, panels)
            for k in range(cap):
                buffer[b, owner * cap + k] = source[meta[base + owner * cap + k]]
            spread_copy(b, buffer, target, send, recv, owner).start()
            return carry

        lax.fori_loop(1, panels, one, 0)

    def add_up(b):
        wait_bytes(got_up[b].at[pl.ds(0, slots - cap)], up_r.at[b])

        def run(j8, acc):
            for i in range(8):
                j = j8 * 8 + i
                acc = jnp.where(meta[m_cont + j] > 0, acc, 0.0) + got_up[b][meta[m_order + j]]
                prefix[j] = acc
            return acc

        lax.fori_loop(0, slots // 8, run, jnp.zeros((ROWS, width), jnp.float32))

        def one(c, carry):
            for i in range(chunk):
                m = c * chunk + i
                sums[b, m] = prefix[meta[m_last + m]]
            up_copy(b, c).start()
            return carry

        lax.fori_loop(0, chunks, one, 0)

    def top(b):
        def one(c, carry):
            wait_bytes(got_sums.at[b, pl.ds(c * chunk, chunk)], z_r.at[b, c])
            for i in range(chunk):
                n = c * chunk + i
                x = times(gbuf[b, n] - got_sums[b, n], inv[n])
                fsol[b, n] = x
                bsol[b, n] = times(x, inv_t[n])
            down_copy(b, c).start()
            return carry

        lax.fori_loop(0, chunks, one, 0)

    def hand_down(b):
        wait_bytes(got_above[b], b_r.at[b])
        spread(b, got_above[b], m_pos, send_down, got_down[b], dn_s, dn_r)

    def backward(b):
        wait_bytes(got_down[b].at[pl.ds(0, slots - cap)], dn_r.at[b])

        def one(c, carry):
            for i in range(chunk):
                n = c * chunk + i
                low = times(got_down[b][meta[m_slot + n]], cpl_t[n])
                bsol[b, n] = times(fsol[b, n] - low, inv_t[n])

            @pl.when(above_bottom)
            def _():
                down_copy(b, c).start()

            return carry

        lax.fori_loop(0, chunks, one, 0)
        out_copy(1, b).start()

    @pl.when(below_top)
    def _():
        for b in range(blocks + 1):
            if b < blocks:
                if b == 0:
                    @pl.when(above_bottom)
                    def _():
                        forward(0)
                else:
                    forward(b)
                spread(b, upd, m_send, send_up, got_up[b], up_s, up_r)
                out_copy(0, b).start()
            if b > 0:
                add_up(b - 1)

        @pl.when(level == 0)
        def _():
            lax.fori_loop(0, nodes, turn, 0)

        for b in range(blocks + 1):
            if b < blocks:
                hand_down(b)
            if b > 0:
                backward(b - 1)
        for b in range(blocks):
            wait_bytes(send_up.at[b, pl.ds(0, slots - cap)], up_s.at[b])
            wait_bytes(send_down.at[b, pl.ds(0, slots - cap)], dn_s.at[b])
            wait_bytes(sums.at[b], z_s.at[b])

    @pl.when(level == levels - 1)
    def _():
        for b in range(blocks):
            if b > 0:
                given_copy(b).wait()
            top(b)
            out_copy(0, b).start()
            out_copy(1, b).start()

    @pl.when(above_bottom)
    def _():
        for b in range(blocks):
            wait_bytes(bsol.at[b], b_s.at[b])

    for b in range(blocks):
        out_copy(0, b).wait()
        out_copy(1, b).wait()


def places(owners, positions, panels, cap):
    nodes = owners.shape[0]
    slots = panels * cap
    i32 = jnp.int32
    node = jnp.arange(nodes, dtype=i32)
    slot = jnp.arange(slots, dtype=i32)
    same = (owners[:, None] == owners[None, :]) & (node[None, :] < node[:, None])
    dest = owners * cap + jnp.sum(same.astype(i32), axis=1)
    hit = slot[:, None] == dest[None, :]
    send = jnp.sum(jnp.where(hit, node[None, :], 0), axis=1)
    ids = nodes - jnp.sum(jnp.where(hit, nodes - positions[None, :], 0), axis=1)
    key = lax.all_to_all(ids, "panel", split_axis=0, concat_axis=0, tiled=True)
    ahead = (key[None, :] < key[:, None]) | ((key[None, :] == key[:, None]) & (slot[None, :] < slot[:, None]))
    rank = jnp.sum(ahead.astype(i32), axis=1)
    placed = rank[None, :] == slot[:, None]
    order = jnp.sum(jnp.where(placed, slot[None, :], 0), axis=1)
    cont = jnp.max(jnp.where(ahead & (key[None, :] == key[:, None]), 1, 0), axis=1)
    cont = jnp.sum(jnp.where(placed, cont[None, :], 0), axis=1)
    mine = key[None, :] == node[:, None]
    last = jnp.max(jnp.where(mine, rank[None, :], -1), axis=1)
    last = jnp.where(last < 0, slots, last)
    return jnp.concatenate([send, order, cont, jnp.minimum(key, nodes - 1), last, dest]).astype(i32)


def body(right_sides, inverse, coupling, owner_map, parent_slot):
    levels = lax.axis_size("leaf")
    panels = lax.axis_size("panel")
    nodes, total_cols, width = right_sides.shape[1:]
    cap = max(2, 2 * nodes // panels)
    slots = panels * cap
    blocks = total_cols // ROWS
    meta = places(owner_map[0, :, 0], parent_slot[0], panels, cap)
    tile = (ROWS, width)
    f32, bf16 = jnp.float32, jnp.bfloat16
    vmem = pltpu.VMEM
    dma = pltpu.SemaphoreType.DMA
    chunks = nodes // ROWS
    scratch = [
        vmem((STAGED * WCHUNK, width, width), f32), vmem((STAGED * WCHUNK, width, width), f32),
        vmem((nodes, 2 * width, width), bf16), vmem((nodes, 2 * width, width), bf16),
        vmem((nodes, 2 * width, width), bf16), vmem((nodes, 2 * width, width), bf16),
        vmem((blocks, nodes) + tile, f32), vmem((blocks, nodes) + tile, f32), vmem((blocks, nodes) + tile, f32),
        vmem((nodes,) + tile, f32), vmem((slots + 1,) + tile, f32),
        vmem((blocks, slots) + tile, f32), vmem((blocks, nodes) + tile, f32), vmem((blocks, nodes) + tile, f32),
        vmem((blocks, slots) + tile, f32),
    ]
    scratch += [vmem((slots,) + tile, f32) for _ in range(2 * blocks)]
    scratch += [vmem((nodes,) + tile, f32) for _ in range(blocks)]
    scratch += [
        dma((2, nodes // WCHUNK)), dma((blocks,)), dma((2, blocks)),
        dma((blocks,)), dma((blocks,)), dma((blocks,)), dma((blocks, chunks)),
        dma((blocks,)), dma((blocks,)), dma((blocks,)), dma((blocks,)),
    ]
    out = jax.ShapeDtypeStruct(right_sides.shape, f32)
    anywhere = pl.BlockSpec(memory_space=pl.ANY)
    return pl.pallas_call(
        functools.partial(kernel, levels, panels, nodes, blocks, width, cap),
        out_shape=(out, out),
        in_specs=[pl.BlockSpec(memory_space=pltpu.SMEM), anywhere, anywhere, anywhere],
        out_specs=(anywhere, anywhere),
        scratch_shapes=scratch,
        compiler_params=pltpu.CompilerParams(
            collective_id=0, has_side_effects=True, vmem_limit_bytes=60 * 1024 * 1024
        ),
    )(meta, right_sides, inverse, coupling)


def solution(mesh):
    in_specs = (
        P("leaf", "panel", None, None),
        P("leaf", "panel", None, None),
        P("leaf", "panel", None, None),
        P("leaf", "panel", None),
        P("leaf", "panel"),
    )
    out_specs = (P("leaf", "panel", None, None), P("leaf", "panel", None, None))
    return jax.shard_map(body, mesh=mesh, in_specs=in_specs, out_specs=out_specs, check_vma=False)
```
